256 devices in a mesh: row: 8 (over y, core), col: 32 (over x, z).
Axes of the slice: x: 4, y: 4, z: 8, core: 2. Of those that a mesh axis runs over, the one named last changes fastest.
Arguments:
- pivots: bfloat16 [2, 1024, 128], P(None, ('row', 'col')), may hold values from -4 to 4
- landmarks: bfloat16 [98304, 128], P(('row', 'col')), may hold values from -4 to 4
Outputs:
- low_panel: float32 [98304, 1024], P(('row', 'col'))
- updated_panel: float32 [98304, 1024], P(('row', 'col'))
- next_block: float32 [1024, 1024], P(('row', 'col'))
The draws below stay inside these ranges and needn't reach their ends.
All inputs are finite; a program needn't handle non-finite values.
Results may differ from the reference program's by a relative error of at most 0.0003.
Values may be sent and summed in bfloat16 or wider, within the bound.
No kernel may reach another device: no remote copies, remote signals or barrier semaphores. Data moves between devices by JAX's collectives and lax.ppermute only.
A program may use at most 128 MiB of HBM per device.

```python
import jax
import jax.numpy as jnp
from jax import lax

PANEL = 1024
FEAT = 128
ROWS_DEV = 384
ROWS = 98304


def level_of(own_key, shape, pieces, smallest, largest):
    gain, own = 1.0, jax.random.fold_in(own_key, 6)
    for axis_at, parts in pieces:
        heights = jnp.exp(jax.random.uniform(jax.random.fold_in(own, axis_at), (parts,), jnp.float32, smallest / len(pieces), largest / len(pieces)))
        gain = gain * jnp.repeat(heights, shape[axis_at] // parts).reshape([-1 if axis == axis_at else 1 for axis in range(len(shape))])
    return gain


def normal_values(rng, extent, deviation, reach, cuts=(), kind=jnp.bfloat16):
    drawn = deviation * jax.random.normal(rng, extent, jnp.float32)
    if cuts:
        drawn = drawn * level_of(rng, extent, cuts, -0.22, 0.18)
    return jnp.clip(drawn, -reach, reach).astype(kind)


def setup_inputs(seed: int = 0) -> dict:
    key_list = jax.random.split(jax.random.key(seed), 3)
    pivots = normal_values(key_list[0], (2, PANEL, FEAT), 1.0, 4.0, ((1, 256),))
    landmarks = normal_values(key_list[1], (ROWS, FEAT), 1.0, 4.0, ((0, 256),))
    return {"pivots": pivots, "landmarks": landmarks}


ridge = 1.0

def kernel(left_rows, right_rows):
    cross = jnp.dot(left_rows.astype(jnp.float32), right_rows.T.astype(jnp.float32), preferred_element_type=jnp.float32)
    left_sq = jnp.sum(jnp.square(left_rows.astype(jnp.float32)), axis=1)
    right_sq = jnp.sum(jnp.square(right_rows.astype(jnp.float32)), axis=1)
    return jnp.exp(-(left_sq[:, None] + right_sq[None, :] - 2.0 * cross) / FEAT)

def reference(pivots, landmarks):
    identity = jnp.eye(PANEL, dtype=jnp.float32)
    first_piv = pivots[0]
    second_piv = pivots[1]
    diagonal_block = kernel(first_piv, first_piv) + ridge * identity
    factor = jnp.linalg.cholesky(diagonal_block)
    inverse = jax.scipy.linalg.solve_triangular(factor, identity, lower=True)
    inverse_t = inverse.T
    pivot_panel = jnp.dot(kernel(second_piv, first_piv), inverse_t, precision=lax.Precision.HIGHEST)
    next_block = kernel(second_piv, second_piv) + ridge * identity - jnp.dot(pivot_panel, pivot_panel.T, precision=lax.Precision.HIGHEST)
    all_pivots = pivots.reshape(2 * PANEL, FEAT)

    def one_block(rows):
        kernels = kernel(rows, all_pivots)
        solved = jnp.dot(kernels[:, :PANEL], inverse_t, precision=lax.Precision.HIGHEST)
        updated = kernels[:, PANEL:] - jnp.dot(solved, pivot_panel.T, precision=lax.Precision.HIGHEST)
        return (solved, updated)
    solved, updated = lax.map(one_block, landmarks.reshape(-1, ROWS_DEV, FEAT))
    return (solved.reshape(ROWS, PANEL), updated.reshape(ROWS, PANEL), next_block)
```

```python
import jax
import jax.numpy as jnp
from jax import lax
from jax.experimental import pallas as pl
from jax.experimental.pallas import tpu as pltpu
from jax.sharding import PartitionSpec as P

FEAT = 128
PANEL = 1024
RIDGE = 1.0
SUB = 8
LANES = 128
INNER = 128
OUTER = 256
f32 = jnp.float32
bf16 = jnp.bfloat16


def split(x):
    high = x.astype(bf16)
    return high, (x - high.astype(f32)).astype(bf16)


def dot_t(a, b):
    return lax.dot_general(a, b, (((1,), (1,)), ((), ())), preferred_element_type=f32)


def dot_n(a, b):
    return jnp.dot(a, b, preferred_element_type=f32)


def product(dot, a, b):
    return dot(a[0], b[0]) + (dot(a[0], b[1]) + dot(a[1], b[0]))


def over_lanes(x, column):
    return jnp.broadcast_to(x[:, column:column + 1], (SUB, LANES))


def over_rows(x, row):
    return jnp.broadcast_to(x[row:row + 1, :], (SUB, LANES))


def inverse_factor(block):
    rows_in_tile = lax.broadcasted_iota(jnp.int32, (SUB, LANES), 0)
    lane = lax.broadcasted_iota(jnp.int32, (SUB, LANES), 1)
    tiles = INNER // SUB
    rows = [block[SUB * t:SUB * (t + 1), :] for t in range(tiles)]
    found = []
    for t in range(tiles):
        first = SUB * t
        columns = [over_lanes(rows[t], first + m) for m in range(SUB)]
        here = (lane >= first) & (lane < first + SUB)
        current = jnp.where(here, jnp.where(lane - first == rows_in_tile, 1.0, 0.0), rows[t])
        scaled = jnp.zeros((SUB, LANES), f32)
        for k in range(SUB):
            pivot = over_rows(columns[k], k)
            inverse = 1.0 / pivot
            pivot_row = over_rows(current, k)
            scaled = jnp.where(rows_in_tile == k, pivot_row * lax.rsqrt(pivot), scaled)
            factors = jnp.where(rows_in_tile == k, 1.0 - inverse, columns[k] * inverse)
            current = current - factors * pivot_row
            for m in range(k + 1, SUB):
                columns[m] = columns[m] - factors * over_rows(columns[m], k)
        found.append(jnp.where(lane <= first + rows_in_tile, scaled, 0.0))
        pivots = [over_rows(current, m) for m in range(SUB)]
        for s in range(t + 1, tiles):
            terms = [over_lanes(rows[s], first + m) * pivots[m] for m in range(SUB)]
            while len(terms) > 1:
                terms = [a + b for a, b in zip(terms[::2], terms[1::2])]
            rows[s] = jnp.where(here, 0.0, rows[s]) - terms[0]
    return jnp.concatenate(found, axis=0)


def squares(x):
    x = x.astype(f32)
    return jnp.sum(x * x, axis=1, keepdims=True)


def squares_along_lanes(x):
    x = x.astype(f32)
    high, low = split(x * x)
    ones = jnp.ones((16, FEAT), bf16)
    return (dot_t(ones, high) + dot_t(ones, low))[:1]


def kernel_values(left, left_sq, right, right_sq):
    return jnp.exp((2.0 * dot_t(left, right) - left_sq - right_sq) * (1.0 / FEAT))


def local_body(local_rows, pivots_ref, left_ref, low_ref, updated_ref, next_ref,
               panel, bottom, panel_high, panel_low, bottom_high, bottom_low, right_kernels):
    own_rows = next_ref.shape[0]
    offset = lax.axis_index(("row", "col")) * own_rows
    left_count = left_ref.shape[0]
    first = pivots_ref[:PANEL, :]
    first_lanes = squares_along_lanes(first)
    chunk = OUTER
    chunks = [(at, chunk) for at in range(0, PANEL, chunk)]
    bottom_chunks = chunks + [(PANEL, left_count)]

    def rows_of(at, count):
        return left_ref[...] if at == PANEL else pivots_ref[pl.ds(PANEL + at, count), :]

    for at, count in chunks:
        x = pivots_ref[at:at + count, :]
        values = kernel_values(x, squares(x), first, first_lanes)
        row = lax.broadcasted_iota(jnp.int32, values.shape, 0) + at
        column = lax.broadcasted_iota(jnp.int32, values.shape, 1)
        panel[at:at + count, :] = values + jnp.where(row == column, RIDGE, 0.0)
    for at, count in bottom_chunks:
        x = rows_of(at, count)
        bottom[at:at + count, :] = kernel_values(x, squares(x), first, first_lanes)
    second = pivots_ref[PANEL:, :]
    x = left_ref[...]
    right_kernels[...] = kernel_values(x, squares(x), second, squares_along_lanes(second))

    for step in range(PANEL // OUTER):
        at = step * OUTER
        columns = slice(at, at + OUTER)
        mid = at + INNER
        end = at + OUTER
        if step:
            right = (panel_high[columns, :at], panel_low[columns, :at])
            for start, count in chunks[step:]:
                rows = slice(start, start + count)
                left = (panel_high[rows, :at], panel_low[rows, :at])
                panel[rows, columns] = panel[rows, columns] - product(dot_t, left, right)
            for start, count in bottom_chunks:
                rows = slice(start, start + count)
                left = (bottom_high[rows, :at], bottom_low[rows, :at])
                bottom[rows, columns] = bottom[rows, columns] - product(dot_t, left, right)
        upper = inverse_factor(panel[at:mid, at:mid])
        upper_parts = split(upper)
        across = product(dot_t, split(panel[mid:end, at:mid]), upper_parts)
        across_parts = split(across)
        lower = inverse_factor(panel[mid:end, mid:end] - product(dot_t, across_parts, across_parts))
        corner = -product(dot_n, split(lower), split(product(dot_n, across_parts, upper_parts)))
        inverse = jnp.concatenate([
            jnp.concatenate([upper, jnp.zeros((INNER, INNER), f32)], axis=1),
            jnp.concatenate([corner, lower], axis=1)], axis=0)
        inverse = split(inverse)
        for start, count in chunks[step + 1:]:
            rows = slice(start, start + count)
            solved = product(dot_t, split(panel[rows, columns]), inverse)
            panel_high[rows, columns], panel_low[rows, columns] = split(solved)
        for start, count in bottom_chunks:
            rows = slice(start, start + count)
            solved = product(dot_t, split(bottom[rows, columns]), inverse)
            bottom_high[rows, columns], bottom_low[rows, columns] = split(solved)
            if start == PANEL:
                low_ref[:, columns] = solved[:local_rows]

    left = (bottom_high[PANEL:, :], bottom_low[PANEL:, :])
    for start, count in chunks:
        rows = slice(start, start + count)
        right = (bottom_high[rows, :], bottom_low[rows, :])
        values = right_kernels[:, rows] - product(dot_t, left, right)
        updated_ref[:, rows] = values[:local_rows]
        own = values[local_rows:local_rows + own_rows]
        row = lax.broadcasted_iota(jnp.int32, own.shape, 0) + offset
        column = lax.broadcasted_iota(jnp.int32, own.shape, 1) + start
        next_ref[:, rows] = own + jnp.where(row == column, RIDGE, 0.0)


def local_call(pivots, left, local_rows, own_rows):
    left_count = left.shape[0]
    body = lambda *refs: local_body(local_rows, *refs)
    total = PANEL + left_count
    return pl.pallas_call(
        body,
        out_shape=(
            jax.ShapeDtypeStruct((local_rows, PANEL), f32),
            jax.ShapeDtypeStruct((local_rows, PANEL), f32),
            jax.ShapeDtypeStruct((own_rows, PANEL), f32),
        ),
        scratch_shapes=[
            pltpu.VMEM((PANEL, PANEL), f32),
            pltpu.VMEM((total, PANEL), f32),
            pltpu.VMEM((PANEL, PANEL), bf16),
            pltpu.VMEM((PANEL, PANEL), bf16),
            pltpu.VMEM((total, PANEL), bf16),
            pltpu.VMEM((total, PANEL), bf16),
            pltpu.VMEM((left_count, PANEL), f32),
        ],
        compiler_params=pltpu.CompilerParams(vmem_limit_bytes=56 * 1024 * 1024),
        name="panels",
    )(pivots, left)


def body(pivots, landmarks):
    axes = ("row", "col")
    devices = lax.axis_size(axes)
    own_count, feat = pivots.shape[1:]
    local_rows = landmarks.shape[0]
    copies = jnp.broadcast_to(pivots[None], (devices,) + pivots.shape)
    gathered = lax.all_to_all(copies, axes, 0, 0, tiled=True)
    everyone = gathered.transpose(1, 0, 2, 3).reshape(2 * devices * own_count, feat)
    padding = jnp.zeros((16 - own_count, feat), landmarks.dtype)
    left = jnp.concatenate([landmarks, pivots[1], padding], axis=0)
    return local_call(everyone, left, local_rows, own_count)


def solution(mesh):
    in_specs = (P(None, ("row", "col"), None), P(("row", "col"), None))
    out_specs = (P(("row", "col"), None), P(("row", "col"), None), P(("row", "col"), None))
    return jax.shard_map(body, mesh=mesh, in_specs=in_specs, out_specs=out_specs, check_vma=False)
```

```python
import jax
import jax.numpy as jnp
from jax import lax
from jax.experimental import pallas as pl
from jax.experimental.pallas import tpu as pltpu
from jax.sharding import PartitionSpec as P

FEAT = 128
PANEL = 1024
RIDGE = 1.0
SUB = 8
LANES = 128
INNER = 128
OUTER = 256
WINDOW = 4
NEAR = 3
CORES = 2
f32 = jnp.float32
bf16 = jnp.bfloat16


def split(x):
    high = x.astype(bf16)
    return high, (x - high.astype(f32)).astype(bf16)


def dot_t(a, b):
    return lax.dot_general(a, b, (((1,), (1,)), ((), ())), preferred_element_type=f32)


def dot_n(a, b):
    return jnp.dot(a, b, preferred_element_type=f32)


def product(dot, a, b):
    return dot(a[0], b[0]) + (dot(a[0], b[1]) + dot(a[1], b[0]))


def over_lanes(x, column):
    return jnp.broadcast_to(x[:, column:column + 1], (SUB, LANES))


def over_rows(x, row):
    return jnp.broadcast_to(x[row:row + 1, :], (SUB, LANES))


def total_of(terms):
    terms = list(terms)
    while len(terms) > 1:
        terms = [a + b for a, b in zip(terms[::2], terms[1::2])] + terms[len(terms) // 2 * 2:]
    return terms[0]


def inverse_factor(block, work=()):
    work = list(work)
    rows_in_tile = lax.broadcasted_iota(jnp.int32, (SUB, LANES), 0)
    lane = lax.broadcasted_iota(jnp.int32, (SUB, LANES), 1)
    is_row = [rows_in_tile == k for k in range(SUB)]
    tiles = INNER // SUB
    rows = [block[SUB * t:SUB * (t + 1), :] for t in range(tiles)]
    found = []
    pivots = [over_lanes(rows[0], m) for m in range(SUB)]
    share = len(work) / tiles
    done = 0
    for t in range(tiles):
        first = SUB * t
        after = first + SUB
        last = t == tiles - 1
        opened = t // WINDOW * WINDOW
        limit = opened + WINDOW + NEAR
        limit = tiles if limit + 1 >= tiles else limit
        if not last:
            following = [over_lanes(rows[t], after + m) for m in range(SUB)]
            below = [over_lanes(rows[t + 1], first + m) for m in range(SUB)]
            coming = [over_lanes(rows[t + 1], after + m) for m in range(SUB)]
        here = (lane >= first) & (lane < after)
        current = jnp.where(here, jnp.where(lane - first == rows_in_tile, 1.0, 0.0), rows[t])
        scaled = None
        for k in range(SUB):
            pivot = over_rows(pivots[k], k)
            inverse = 1.0 / pivot
            column = jnp.where(is_row[k], -1.0, pivots[k])
            for m in range(k + 1, SUB):
                row = over_rows(pivots[m], k)
                pivots[m] = jnp.where(is_row[k], 0.0, pivots[m]) - (column * row) * inverse
            factors = column * inverse
            row = over_rows(current, k)
            taken = row * lax.rsqrt(pivot)
            scaled = taken if scaled is None else jnp.where(rows_in_tile >= k, taken, scaled)
            current = jnp.where(is_row[k], 0.0, current) - factors * row
            if not last:
                for m in range(SUB):
                    row = over_rows(following[m], k)
                    following[m] = jnp.where(is_row[k], 0.0, following[m]) - factors * row
        found.append(scaled)
        while done < min(len(work), round((t + 1) * share)):
            work[done]()
            done += 1
        if last:
            break
        pivots = [coming[m] - total_of([below[i] * over_rows(following[m], i) for i in range(SUB)])
                  for m in range(SUB)]
        spread = [over_rows(current, m) for m in range(SUB)]
        for s in range(t + 1, limit):
            columns = below if s == t + 1 else [over_lanes(rows[s], first + m) for m in range(SUB)]
            rows[s] = jnp.where(here, 0.0, rows[s]) - total_of(
                [columns[m] * spread[m] for m in range(SUB)])
        if (t + 1) % WINDOW == 0 and limit < tiles:
            window = jnp.concatenate(found[opened:], axis=0)
            rank = lax.broadcasted_iota(jnp.int32, window.shape, 0) + SUB * opened
            place = lax.broadcasted_iota(jnp.int32, window.shape, 1)
            left = split(window.T[SUB * limit:, :])
            window = jnp.where((place > rank) & (place < after), 0.0, window)
            change = product(dot_n, left, split(window))
            inside = (lane >= SUB * opened) & (lane < after)
            for s in range(limit, tiles):
                at = SUB * (s - limit)
                rows[s] = jnp.where(inside, 0.0, rows[s]) - change[at:at + SUB, :]
    return jnp.concatenate([jnp.where(lane <= SUB * t + rows_in_tile, x, 0.0)
                            for t, x in enumerate(found)], axis=0)


def squares(x):
    x = x.astype(f32)
    return jnp.sum(x * x, axis=1, keepdims=True)


def squares_along_lanes(x):
    x = x.astype(f32)
    high, low = split(x * x)
    ones = jnp.ones((16, FEAT), bf16)
    return (dot_t(ones, high) + dot_t(ones, low))[:1]


def kernel_values(left, left_sq, right, right_sq):
    return jnp.exp((2.0 * dot_t(left, right) - left_sq - right_sq) * (1.0 / FEAT))


def arrange_pivots(source_ref, pivots_ref, core):
    chips = lax.axis_size("row") // CORES
    columns = source_ref.shape[0] // chips
    count = columns * SUB // 2
    row = lax.broadcasted_iota(jnp.int32, (columns // 2, SUB, FEAT), 1)
    for y in range(chips):
        x = source_ref[columns * y:columns * (y + 1)].astype(f32).reshape(columns // 2, 2, SUB, FEAT)
        even, odd = x[:, 0], x[:, 1]
        first = jnp.where(row < SUB // 2, even, pltpu.roll(odd, SUB // 2, 1))
        second = jnp.where(row < SUB // 2, pltpu.roll(even, SUB // 2, 1), odd)
        at = (y * CORES + core) * count
        for base, value in ((0, first), (PANEL, second)):
            rows = pl.ds(pl.multiple_of(base + at, count), count)
            pivots_ref[rows, :] = value.reshape(count, FEAT).astype(bf16)


def local_body(own_ref, same_ref, other_ref, landmarks_ref, low_ref, updated_ref, next_ref,
               panel, bottom, panel_high, panel_low, bottom_high, bottom_low, right_kernels,
               inverse_high, inverse_low, pivots_ref, left_ref):
    local_rows = landmarks_ref.shape[0]
    own_rows = next_ref.shape[0]
    offset = lax.axis_index(("row", "col")) * own_rows
    core = lax.axis_index("row") % CORES
    arrange_pivots(same_ref, pivots_ref, core)
    arrange_pivots(other_ref, pivots_ref, 1 - core)
    left_count = left_ref.shape[0]
    left_ref[:local_rows, :] = landmarks_ref[...]
    padding = jnp.zeros((left_count - local_rows - own_rows, FEAT), f32)
    left_ref[local_rows:, :] = jnp.concatenate(
        [own_ref[1].astype(f32), padding], axis=0).astype(bf16)
    first = pivots_ref[:PANEL, :]
    first_lanes = squares_along_lanes(first)
    chunks = [slice(at, at + OUTER) for at in range(0, PANEL, OUTER)]
    part = OUTER
    bottom_chunks = [slice(at, at + part) for at in range(0, PANEL, part)]
    bottom_chunks.append(slice(PANEL, PANEL + left_count))

    def panel_values(rows):
        x = pivots_ref[rows, :]
        width = rows.stop
        values = kernel_values(x, squares(x), first[:width], first_lanes[:, :width])
        row = lax.broadcasted_iota(jnp.int32, values.shape, 0) + rows.start
        column = lax.broadcasted_iota(jnp.int32, values.shape, 1)
        panel[rows, :width] = values + jnp.where(row == column, RIDGE, 0.0)

    def bottom_values(rows):
        x = left_ref[...] if rows.start == PANEL else pivots_ref[PANEL + rows.start:PANEL + rows.stop, :]
        bottom[rows, :] = kernel_values(x, squares(x), first, first_lanes)

    def right_values(columns):
        x = left_ref[...]
        y = pivots_ref[PANEL + columns.start:PANEL + columns.stop, :]
        right_kernels[:, columns] = kernel_values(x, squares(x), y, squares_along_lanes(y))

    def solve(source, high, low, rows, columns):
        inverse = (inverse_high[...], inverse_low[...])
        solved = product(dot_t, split(source[rows, columns]), inverse)
        high[rows, columns], low[rows, columns] = split(solved)
        if rows.start == PANEL:
            low_ref[:, columns] = solved[:local_rows]

    def reduce(target, high, low, rows, columns):
        done = slice(0, columns.start)
        right = (panel_high[columns, done], panel_low[columns, done])
        left = (high[rows, done], low[rows, done])
        target[rows, columns] = target[rows, columns] - product(dot_t, left, right)

    def update(at, columns):
        left = (bottom_high[PANEL:, at], bottom_low[PANEL:, at])
        right = (bottom_high[columns, at], bottom_low[columns, at])
        values = right_kernels[:, columns] - product(dot_t, left, right)
        if at.stop < PANEL:
            right_kernels[:, columns] = values
            return
        updated_ref[:, columns] = values[:local_rows]
        own = values[local_rows:local_rows + own_rows]
        row = lax.broadcasted_iota(jnp.int32, own.shape, 0) + offset
        column = lax.broadcasted_iota(jnp.int32, own.shape, 1) + columns.start
        next_ref[:, columns] = own + jnp.where(row == column, RIDGE, 0.0)

    def later(call, *operands):
        return lambda: call(*operands)

    panel_values(chunks[0])
    for step, columns in enumerate(chunks):
        at, mid, end = columns.start, columns.start + INNER, columns.stop
        work = []
        if step == 0:
            work += [later(panel_values, rows) for rows in chunks[1:]]
            work += [later(bottom_values, rows) for rows in bottom_chunks]
            work += [later(right_values, block) for block in chunks]
        else:
            before = chunks[step - 1]
            reduce(panel, panel_high, panel_low, columns, columns)
            work += [later(solve, panel, panel_high, panel_low, rows, before)
                     for rows in chunks[step + 1:]]
            work += [later(reduce, panel, panel_high, panel_low, rows, columns)
                     for rows in chunks[step + 1:]]
            work += [later(solve, bottom, bottom_high, bottom_low, rows, before)
                     for rows in bottom_chunks]
            work += [later(update, before, block) for block in chunks]
            work += [later(reduce, bottom, bottom_high, bottom_low, rows, columns)
                     for rows in bottom_chunks]
        half = len(work) // 2
        upper = inverse_factor(panel[at:mid, at:mid], work[:half])
        upper_parts = split(upper)
        across = product(dot_t, split(panel[mid:end, at:mid]), upper_parts)
        across_parts = split(across)
        lower = inverse_factor(
            panel[mid:end, mid:end] - product(dot_t, across_parts, across_parts), work[half:])
        corner = -product(dot_n, split(lower), split(product(dot_n, across_parts, upper_parts)))
        inverse = jnp.concatenate([
            jnp.concatenate([upper, jnp.zeros((INNER, INNER), f32)], axis=1),
            jnp.concatenate([corner, lower], axis=1)], axis=0)
        inverse_high[...], inverse_low[...] = split(inverse)
        if step + 1 < len(chunks):
            solve(panel, panel_high, panel_low, chunks[step + 1], columns)
    for rows in bottom_chunks:
        solve(bottom, bottom_high, bottom_low, rows, chunks[-1])
    for block in chunks:
        update(chunks[-1], block)


def local_call(own, same, other, landmarks):
    own_rows = own.shape[1]
    local_rows = landmarks.shape[0]
    left_count = local_rows + 2 * SUB
    total = PANEL + left_count
    return pl.pallas_call(
        local_body,
        out_shape=(
            jax.ShapeDtypeStruct((local_rows, PANEL), f32),
            jax.ShapeDtypeStruct((local_rows, PANEL), f32),
            jax.ShapeDtypeStruct((own_rows, PANEL), f32),
        ),
        scratch_shapes=[
            pltpu.VMEM((PANEL, PANEL), f32),
            pltpu.VMEM((total, PANEL), f32),
            pltpu.VMEM((PANEL, PANEL), bf16),
            pltpu.VMEM((PANEL, PANEL), bf16),
            pltpu.VMEM((total, PANEL), bf16),
            pltpu.VMEM((total, PANEL), bf16),
            pltpu.VMEM((left_count, PANEL), f32),
            pltpu.VMEM((OUTER, OUTER), bf16),
            pltpu.VMEM((OUTER, OUTER), bf16),
            pltpu.VMEM((2 * PANEL, FEAT), bf16),
            pltpu.VMEM((left_count, FEAT), bf16),
        ],
        compiler_params=pltpu.CompilerParams(vmem_limit_bytes=56 * 1024 * 1024),
        name="panels",
    )(own, same, other, landmarks)


def body(pivots, landmarks):
    own_count, feat = pivots.shape[1:]
    rows, columns = lax.axis_size("row"), lax.axis_size("col")
    chips = rows // CORES
    own = pivots.reshape(2 * own_count, feat)
    groups = [[(y * CORES + core) * columns + c for y in range(chips) for c in range(columns)]
              for core in range(CORES)]
    copies = jnp.broadcast_to(own[None], (chips * columns,) + own.shape)
    same = lax.all_to_all(copies, ("row", "col"), 0, 0, axis_index_groups=groups, tiled=True)
    other = lax.ppermute(same, "row", [(i, i ^ 1) for i in range(rows)])
    return local_call(pivots, same, other, landmarks)


def solution(mesh):
    in_specs = (P(None, ("row", "col"), None), P(("row", "col"), None))
    out_specs = (P(("row", "col"), None), P(("row", "col"), None), P(("row", "col"), None))
    return jax.shard_map(body, mesh=mesh, in_specs=in_specs, out_specs=out_specs, check_vma=False)
```

```python
import jax
import jax.numpy as jnp
from jax import lax
from jax.experimental import pallas as pl
from jax.experimental.pallas import tpu as pltpu
from jax.sharding import PartitionSpec as P

FEAT = 128
PANEL = 1024
RIDGE = 1.0
SUB = 8
LANES = 128
INNER = 128
OUTER = 256
WINDOW = 4
NEAR = 3
CORES = 2
f32 = jnp.float32
bf16 = jnp.bfloat16


def split(x):
    high = x.astype(bf16)
    return high, (x - high.astype(f32)).astype(bf16)


def dot_t(a, b):
    return lax.dot_general(a, b, (((1,), (1,)), ((), ())), preferred_element_type=f32)


def dot_n(a, b):
    return jnp.dot(a, b, preferred_element_type=f32)


def product(dot, a, b):
    return dot(a[0], b[0]) + (dot(a[0], b[1]) + dot(a[1], b[0]))


def over_lanes(x, column):
    return jnp.broadcast_to(x[:, column:column + 1], (SUB, LANES))


def over_rows(x, row):
    return jnp.broadcast_to(x[row:row + 1, :], (SUB, LANES))


def total_of(terms):
    terms = list(terms)
    while len(terms) > 1:
        terms = [a + b for a, b in zip(terms[::2], terms[1::2])] + terms[len(terms) // 2 * 2:]
    return terms[0]


def inverse_factor(block, work=()):
    work = list(work)
    rows_in_tile = lax.broadcasted_iota(jnp.int32, (SUB, LANES), 0)
    lane = lax.broadcasted_iota(jnp.int32, (SUB, LANES), 1)
    is_row = [rows_in_tile == k for k in range(SUB)]
    tiles = INNER // SUB
    rows = [block[SUB * t:SUB * (t + 1), :] for t in range(tiles)]
    found = []
    pivots = [over_lanes(rows[0], m) for m in range(SUB)]
    share = len(work) / tiles
    done = 0
    for t in range(tiles):
        first = SUB * t
        after = first + SUB
        last = t == tiles - 1
        opened = t // WINDOW * WINDOW
        limit = opened + WINDOW + NEAR
        limit = tiles if limit + 1 >= tiles else limit
        if not last:
            following = [over_lanes(rows[t], after + m) for m in range(SUB)]
            below = [over_lanes(rows[t + 1], first + m) for m in range(SUB)]
            coming = [over_lanes(rows[t + 1], after + m) for m in range(SUB)]
        here = (lane >= first) & (lane < after)
        current = jnp.where(here, jnp.where(lane - first == rows_in_tile, 1.0, 0.0), rows[t])
        scaled = None
        for k in range(SUB):
            pivot = over_rows(pivots[k], k)
            inverse = 1.0 / pivot
            column = jnp.where(is_row[k], -1.0, pivots[k])
            for m in range(k + 1, SUB):
                row = over_rows(pivots[m], k)
                pivots[m] = jnp.where(is_row[k], 0.0, pivots[m]) - (column * row) * inverse
            factors = column * inverse
            row = over_rows(current, k)
            taken = row * lax.rsqrt(pivot)
            scaled = taken if scaled is None else jnp.where(rows_in_tile >= k, taken, scaled)
            current = jnp.where(is_row[k], 0.0, current) - factors * row
            if not last:
                for m in range(SUB):
                    row = over_rows(following[m], k)
                    following[m] = jnp.where(is_row[k], 0.0, following[m]) - factors * row
        found.append(scaled)
        while done < min(len(work), round((t + 1) * share)):
            work[done]()
            done += 1
        if last:
            break
        pivots = [coming[m] - total_of([below[i] * over_rows(following[m], i) for i in range(SUB)])
                  for m in range(SUB)]
        spread = [over_rows(current, m) for m in range(SUB)]
        for s in range(t + 1, limit):
            columns = below if s == t + 1 else [over_lanes(rows[s], first + m) for m in range(SUB)]
            rows[s] = jnp.where(here, 0.0, rows[s]) - total_of(
                [columns[m] * spread[m] for m in range(SUB)])
        if (t + 1) % WINDOW == 0 and limit < tiles:
            window = jnp.concatenate(found[opened:], axis=0)
            rank = lax.broadcasted_iota(jnp.int32, window.shape, 0) + SUB * opened
            place = lax.broadcasted_iota(jnp.int32, window.shape, 1)
            left = split(window.T[SUB * limit:, :])
            window = jnp.where((place > rank) & (place < after), 0.0, window)
            change = product(dot_n, left, split(window))
            inside = (lane >= SUB * opened) & (lane < after)
            for s in range(limit, tiles):
                at = SUB * (s - limit)
                rows[s] = jnp.where(inside, 0.0, rows[s]) - change[at:at + SUB, :]
    return jnp.concatenate([jnp.where(lane <= SUB * t + rows_in_tile, x, 0.0)
                            for t, x in enumerate(found)], axis=0)


def squares(x):
    x = x.astype(f32)
    return jnp.sum(x * x, axis=1, keepdims=True)


def squares_along_lanes(x):
    x = x.astype(f32)
    high, low = split(x * x)
    ones = jnp.ones((16, FEAT), bf16)
    return (dot_t(ones, high) + dot_t(ones, low))[:1]


def kernel_values(left, left_sq, right, right_sq):
    return jnp.exp((2.0 * dot_t(left, right) - left_sq - right_sq) * (1.0 / FEAT))


def local_body(own_ref, same_ref, other_ref, landmarks_ref, low_ref, updated_ref, next_ref,
               panel, bottom, panel_high, panel_low, bottom_high, bottom_low, right_kernels,
               inverse_high, inverse_low, pivots_ref, left_ref, lane_squares):
    local_rows = landmarks_ref.shape[0]
    own_rows = next_ref.shape[0]
    offset = lax.axis_index(("row", "col")) * own_rows
    left_count = left_ref.shape[0]
    chunks = [slice(at, at + OUTER) for at in range(0, PANEL, OUTER)]
    bottom_chunks = chunks + [slice(PANEL, PANEL + left_count)]
    chips = lax.axis_size("row") // CORES
    columns_of_mesh = same_ref.shape[0] // chips
    first_core = lax.axis_index("row") % CORES == 0

    def arrange(y):
        count = columns_of_mesh * SUB // 2
        row = lax.broadcasted_iota(jnp.int32, (columns_of_mesh // 2, SUB, FEAT), 1)
        held = slice(columns_of_mesh * y, columns_of_mesh * (y + 1))
        same, other = same_ref[held].astype(f32), other_ref[held].astype(f32)
        by_core = (jnp.where(first_core, same, other), jnp.where(first_core, other, same))
        for core, x in enumerate(by_core):
            x = x.reshape(columns_of_mesh // 2, 2, SUB, FEAT)
            even, odd = x[:, 0], x[:, 1]
            first = jnp.where(row < SUB // 2, even, pltpu.roll(odd, SUB // 2, 1))
            second = jnp.where(row < SUB // 2, pltpu.roll(even, SUB // 2, 1), odd)
            at = (y * CORES + core) * count
            pivots_ref[at:at + count, :] = first.reshape(count, FEAT).astype(bf16)
            pivots_ref[PANEL + at:PANEL + at + count, :] = second.reshape(count, FEAT).astype(bf16)

    def arrange_left():
        left_ref[:local_rows, :] = landmarks_ref[...]
        padding = jnp.zeros((left_count - local_rows - own_rows, FEAT), f32)
        left_ref[local_rows:, :] = jnp.concatenate(
            [own_ref[1].astype(f32), padding], axis=0).astype(bf16)

    def panel_values(rows):
        x = pivots_ref[rows, :]
        lane_squares[:, rows] = squares_along_lanes(x)
        width = rows.stop
        values = kernel_values(x, squares(x), pivots_ref[:width, :], lane_squares[:, :width])
        row = lax.broadcasted_iota(jnp.int32, values.shape, 0) + rows.start
        column = lax.broadcasted_iota(jnp.int32, values.shape, 1)
        panel[rows, :width] = values + jnp.where(row == column, RIDGE, 0.0)

    def bottom_values(rows):
        x = left_ref[...] if rows.start == PANEL else pivots_ref[PANEL + rows.start:PANEL + rows.stop, :]
        bottom[rows, :] = kernel_values(x, squares(x), pivots_ref[:PANEL, :], lane_squares[...])

    def right_values(columns):
        x = left_ref[...]
        y = pivots_ref[PANEL + columns.start:PANEL + columns.stop, :]
        right_kernels[:, columns] = kernel_values(x, squares(x), y, squares_along_lanes(y))

    def solve(source, high, low, rows, columns):
        inverse = (inverse_high[...], inverse_low[...])
        solved = product(dot_t, split(source[rows, columns]), inverse)
        high[rows, columns], low[rows, columns] = split(solved)
        if rows.start == PANEL:
            low_ref[:, columns] = solved[:local_rows]

    def reduce(target, high, low, rows, columns, stop, parts=False):
        right = (panel_high[columns, :stop], panel_low[columns, :stop])
        left = (high[rows, :stop], low[rows, :stop])
        values = target[rows, columns] - product(dot_t, left, right)
        if parts:
            high[rows, columns], low[rows, columns] = split(values)
        else:
            target[rows, columns] = values

    def update(at, columns):
        left = (bottom_high[PANEL:, at], bottom_low[PANEL:, at])
        right = (bottom_high[columns, at], bottom_low[columns, at])
        right_kernels[:, columns] = right_kernels[:, columns] - product(dot_t, left, right)

    def later(call, *operands):
        return lambda: call(*operands)

    def assemble(upper, across, lower):
        corner = -product(dot_n, lower, split(product(dot_n, across, upper)))
        low_half, high_half = slice(0, INNER), slice(INNER, OUTER)
        for ref, part, up, down in zip((inverse_high, inverse_low), split(corner), upper, lower):
            ref[low_half, low_half] = up
            ref[low_half, high_half] = jnp.zeros((INNER, INNER), bf16)
            ref[high_half, low_half] = part
            ref[high_half, high_half] = down

    def head_of_next(rows, left_half, right_half, upper, across):
        solved = split(product(dot_t, split(panel[rows, left_half]), upper))
        panel_high[rows, left_half], panel_low[rows, left_half] = solved
        panel[rows, right_half] = panel[rows, right_half] - product(dot_t, solved, across)
        panel[rows, rows] = panel[rows, rows] - product(dot_t, solved, solved)

    def rest_of_next(rows, half, right_half, lower, top):
        solved = split(product(dot_t, split(panel[rows, right_half]), lower))
        panel_high[rows, right_half], panel_low[rows, right_half] = solved
        panel[rows, half] = panel[rows, half] - product(dot_t, solved, top)
        panel[rows, rows] = panel[rows, rows] - product(dot_t, solved, solved)

    arrange(0)
    panel_values(chunks[0])
    carried = []
    block = panel[:INNER, :INNER]
    for step, columns in enumerate(chunks):
        at, mid, end = columns.start, columns.start + INNER, columns.stop
        left_half, right_half = slice(at, mid), slice(mid, end)
        final = step + 1 == len(chunks)
        work = list(carried)
        if step == 0:
            for y in range(1, chips):
                work += [later(arrange, y), later(panel_values, chunks[y])]
            work += [arrange_left]
            work += [later(bottom_values, rows) for rows in bottom_chunks]
            ahead = len(work)
            work += [later(right_values, block_columns) for block_columns in chunks]
        else:
            before = chunks[step - 1]
            work += [later(solve, panel, panel_high, panel_low, rows, before)
                     for rows in chunks[step + 1:]]
            work += [later(reduce, panel, panel_high, panel_low, rows, columns, at)
                     for rows in chunks[step + 1:]]
            if not final:
                work += [later(reduce, panel, panel_high, panel_low, chunks[step + 1],
                               chunks[step + 1], at)]
            ahead = len(work)
            work += [later(solve, bottom, bottom_high, bottom_low, rows, before)
                     for rows in bottom_chunks]
            work += [later(update, before, block_columns) for block_columns in chunks]
            work += [later(reduce, bottom, bottom_high, bottom_low, rows, columns, at, final)
                     for rows in bottom_chunks]
        half = max(ahead, len(work) // 2)
        upper = split(inverse_factor(block, work[:half]))
        work = work[half:]
        across = split(product(dot_t, split(panel[right_half, left_half]), upper))
        block = panel[right_half, right_half] - product(dot_t, across, across)
        if not final:
            rows = chunks[step + 1]
            work = [later(head_of_next, rows, left_half, right_half, upper, across)] + work
        lower = split(inverse_factor(block, work))
        carried = [later(assemble, upper, across, lower)]
        if not final:
            top = slice(rows.start, rows.start + INNER)
            rest = slice(rows.start + INNER, rows.stop)
            solved = split(product(dot_t, split(panel[top, right_half]), lower))
            panel_high[top, right_half], panel_low[top, right_half] = solved
            block = panel[top, top] - product(dot_t, solved, solved)
            carried = [later(rest_of_next, rest, top, right_half, lower, solved)] + carried

    assemble(upper, across, lower)
    columns = chunks[-1]
    inverse = (inverse_high[...], inverse_low[...])
    solved = product(dot_t, (bottom_high[PANEL:, columns], bottom_low[PANEL:, columns]), inverse)
    low_ref[:, columns] = solved[:local_rows]
    left = split(product(dot_n, split(solved), inverse))
    for rows in chunks:
        values = right_kernels[:, rows] - product(
            dot_t, left, (bottom_high[rows, columns], bottom_low[rows, columns]))
        updated_ref[:, rows] = values[:local_rows]
        own = values[local_rows:local_rows + own_rows]
        row = lax.broadcasted_iota(jnp.int32, own.shape, 0) + offset
        column = lax.broadcasted_iota(jnp.int32, own.shape, 1) + rows.start
        next_ref[:, rows] = own + jnp.where(row == column, RIDGE, 0.0)


def local_call(own, same, other, landmarks):
    own_rows = own.shape[1]
    local_rows = landmarks.shape[0]
    left_count = local_rows + 2 * SUB
    total = PANEL + left_count
    return pl.pallas_call(
        local_body,
        out_shape=(
            jax.ShapeDtypeStruct((local_rows, PANEL), f32),
            jax.ShapeDtypeStruct((local_rows, PANEL), f32),
            jax.ShapeDtypeStruct((own_rows, PANEL), f32),
        ),
        scratch_shapes=[
            pltpu.VMEM((PANEL, PANEL), f32),
            pltpu.VMEM((total, PANEL), f32),
            pltpu.VMEM((PANEL, PANEL), bf16),
            pltpu.VMEM((PANEL, PANEL), bf16),
            pltpu.VMEM((total, PANEL), bf16),
            pltpu.VMEM((total, PANEL), bf16),
            pltpu.VMEM((left_count, PANEL), f32),
            pltpu.VMEM((OUTER, OUTER), bf16),
            pltpu.VMEM((OUTER, OUTER), bf16),
            pltpu.VMEM((2 * PANEL, FEAT), bf16),
            pltpu.VMEM((left_count, FEAT), bf16),
            pltpu.VMEM((1, PANEL), f32),
        ],
        compiler_params=pltpu.CompilerParams(vmem_limit_bytes=56 * 1024 * 1024),
        name="panels",
    )(own, same, other, landmarks)


def body(pivots, landmarks):
    own_count, feat = pivots.shape[1:]
    rows, columns = lax.axis_size("row"), lax.axis_size("col")
    chips = rows // CORES
    own = pivots.reshape(2 * own_count, feat)
    groups = [[(y * CORES + core) * columns + c for y in range(chips) for c in range(columns)]
              for core in range(CORES)]
    copies = jnp.broadcast_to(own[None], (chips * columns,) + own.shape)
    same = lax.all_to_all(copies, ("row", "col"), 0, 0, axis_index_groups=groups, tiled=True)
    other = lax.ppermute(same, "row", [(i, i ^ 1) for i in range(rows)])
    return local_call(pivots, same, other, landmarks)


def solution(mesh):
    in_specs = (P(None, ("row", "col"), None), P(("row", "col"), None))
    out_specs = (P(("row", "col"), None), P(("row", "col"), None), P(("row", "col"), None))
    return jax.shard_map(body, mesh=mesh, in_specs=in_specs, out_specs=out_specs, check_vma=False)
```

```python
import jax
import jax.numpy as jnp
from jax import lax
from jax.experimental import pallas as pl
from jax.experimental.pallas import tpu as pltpu
from jax.sharding import PartitionSpec as P

FEAT = 128
PANEL = 1024
RIDGE = 1.0
SUB = 8
LANES = 128
INNER = 128
OUTER = 256
WINDOW = 4
NEAR = 3
CORES = 2
f32 = jnp.float32
bf16 = jnp.bfloat16


def split(x):
    high = x.astype(bf16)
    return high, (x - high.astype(f32)).astype(bf16)


def dot_t(a, b):
    return lax.dot_general(a, b, (((1,), (1,)), ((), ())), preferred_element_type=f32)


def dot_n(a, b):
    return jnp.dot(a, b, preferred_element_type=f32)


def product(dot, a, b):
    return dot(a[0], b[0]) + (dot(a[0], b[1]) + dot(a[1], b[0]))


def over_lanes(x, column):
    return jnp.broadcast_to(x[:, column:column + 1], (SUB, LANES))


def over_rows(x, row):
    return jnp.broadcast_to(x[row:row + 1, :], (SUB, LANES))


def total_of(terms):
    terms = list(terms)
    while len(terms) > 1:
        terms = [a + b for a, b in zip(terms[::2], terms[1::2])] + terms[len(terms) // 2 * 2:]
    return terms[0]


def inverse_factor(block, work=()):
    work = list(work)
    rows_in_tile = lax.broadcasted_iota(jnp.int32, (SUB, LANES), 0)
    lane = lax.broadcasted_iota(jnp.int32, (SUB, LANES), 1)
    is_row = [rows_in_tile == k for k in range(SUB)]
    tiles = INNER // SUB
    rows = [block[SUB * t:SUB * (t + 1), :] for t in range(tiles)]
    found = []
    pivots = [over_lanes(rows[0], m) for m in range(SUB)]
    share = len(work) / tiles
    done = 0
    for t in range(tiles):
        first = SUB * t
        after = first + SUB
        last = t == tiles - 1
        opened = t // WINDOW * WINDOW
        limit = opened + WINDOW + NEAR
        limit = tiles if limit + 1 >= tiles else limit
        if not last:
            following = [over_lanes(rows[t], after + m) for m in range(SUB)]
            below = [over_lanes(rows[t + 1], first + m) for m in range(SUB)]
            coming = [over_lanes(rows[t + 1], after + m) for m in range(SUB)]
        here = (lane >= first) & (lane < after)
        current = jnp.where(here, jnp.where(lane - first == rows_in_tile, 1.0, 0.0), rows[t])
        scaled = None
        for k in range(SUB):
            pivot = over_rows(pivots[k], k)
            inverse = 1.0 / pivot
            column = jnp.where(is_row[k], -1.0, pivots[k])
            for m in range(k + 1, SUB):
                row = over_rows(pivots[m], k)
                pivots[m] = jnp.where(is_row[k], 0.0, pivots[m]) - (column * row) * inverse
            factors = column * inverse
            row = over_rows(current, k)
            taken = row * lax.rsqrt(pivot)
            scaled = taken if scaled is None else jnp.where(rows_in_tile >= k, taken, scaled)
            current = jnp.where(is_row[k], 0.0, current) - factors * row
            if not last:
                for m in range(SUB):
                    row = over_rows(following[m], k)
                    following[m] = jnp.where(is_row[k], 0.0, following[m]) - factors * row
        found.append(scaled)
        while done < min(len(work), round((t + 1) * share)):
            work[done]()
            done += 1
        if last:
            break
        pivots = [coming[m] - total_of([below[i] * over_rows(following[m], i) for i in range(SUB)])
                  for m in range(SUB)]
        spread = [over_rows(current, m) for m in range(SUB)]
        for s in range(t + 1, limit):
            columns = below if s == t + 1 else [over_lanes(rows[s], first + m) for m in range(SUB)]
            rows[s] = jnp.where(here, 0.0, rows[s]) - total_of(
                [columns[m] * spread[m] for m in range(SUB)])
        if (t + 1) % WINDOW == 0 and limit < tiles:
            window = jnp.concatenate(found[opened:], axis=0)
            rank = lax.broadcasted_iota(jnp.int32, window.shape, 0) + SUB * opened
            place = lax.broadcasted_iota(jnp.int32, window.shape, 1)
            left = split(window.T[SUB * limit:, :])
            window = jnp.where((place > rank) & (place < after), 0.0, window)
            change = product(dot_n, left, split(window))
            inside = (lane >= SUB * opened) & (lane < after)
            for s in range(limit, tiles):
                at = SUB * (s - limit)
                rows[s] = jnp.where(inside, 0.0, rows[s]) - change[at:at + SUB, :]
    return jnp.concatenate([jnp.where(lane <= SUB * t + rows_in_tile, x, 0.0)
                            for t, x in enumerate(found)], axis=0)


def squares(x):
    x = x.astype(f32)
    return jnp.sum(x * x, axis=1, keepdims=True)


def squares_along_lanes(x):
    x = x.astype(f32)
    high, low = split(x * x)
    ones = jnp.ones((16, FEAT), bf16)
    return (dot_t(ones, high) + dot_t(ones, low))[:1]


def kernel_values(left, left_sq, right, right_sq):
    return jnp.exp((2.0 * dot_t(left, right) - left_sq - right_sq) * (1.0 / FEAT))


def local_body(own_ref, same_ref, other_ref, landmarks_ref, low_out, updated_out, next_ref,
               panel, bottom, panel_high, panel_low, bottom_high, bottom_low, right_kernels,
               inverse_high, inverse_low, pivots_ref, left_ref, lane_squares, low_ref, updated_ref,
               sent):
    local_rows = landmarks_ref.shape[0]
    own_rows = next_ref.shape[0]
    offset = lax.axis_index(("row", "col")) * own_rows
    left_count = left_ref.shape[0]
    chunks = [slice(at, at + OUTER) for at in range(0, PANEL, OUTER)]
    bottom_chunks = chunks + [slice(PANEL, PANEL + left_count)]
    chips = lax.axis_size("row") // CORES
    columns_of_mesh = same_ref.shape[0] // chips
    first_core = lax.axis_index("row") % CORES == 0

    copies = []

    def send(source, target, columns):
        copy = pltpu.make_async_copy(
            source.at[:, columns], target.at[:, columns], sent.at[len(copies)])
        copy.start()
        copies.append(copy)

    def arrange(y):
        count = columns_of_mesh * SUB // 2
        row = lax.broadcasted_iota(jnp.int32, (columns_of_mesh // 2, SUB, FEAT), 1)
        held = slice(columns_of_mesh * y, columns_of_mesh * (y + 1))
        same, other = same_ref[held].astype(f32), other_ref[held].astype(f32)
        by_core = (jnp.where(first_core, same, other), jnp.where(first_core, other, same))
        for core, x in enumerate(by_core):
            x = x.reshape(columns_of_mesh // 2, 2, SUB, FEAT)
            even, odd = x[:, 0], x[:, 1]
            first = jnp.where(row < SUB // 2, even, pltpu.roll(odd, SUB // 2, 1))
            second = jnp.where(row < SUB // 2, pltpu.roll(even, SUB // 2, 1), odd)
            at = (y * CORES + core) * count
            pivots_ref[at:at + count, :] = first.reshape(count, FEAT).astype(bf16)
            pivots_ref[PANEL + at:PANEL + at + count, :] = second.reshape(count, FEAT).astype(bf16)

    def arrange_left():
        left_ref[:local_rows, :] = landmarks_ref[...]
        padding = jnp.zeros((left_count - local_rows - own_rows, FEAT), f32)
        left_ref[local_rows:, :] = jnp.concatenate(
            [own_ref[1].astype(f32), padding], axis=0).astype(bf16)

    def panel_values(rows):
        x = pivots_ref[rows, :]
        lane_squares[:, rows] = squares_along_lanes(x)
        width = rows.stop
        values = kernel_values(x, squares(x), pivots_ref[:width, :], lane_squares[:, :width])
        row = lax.broadcasted_iota(jnp.int32, values.shape, 0) + rows.start
        column = lax.broadcasted_iota(jnp.int32, values.shape, 1)
        panel[rows, :width] = values + jnp.where(row == column, RIDGE, 0.0)

    def bottom_values(rows):
        x = left_ref[...] if rows.start == PANEL else pivots_ref[PANEL + rows.start:PANEL + rows.stop, :]
        bottom[rows, :] = kernel_values(x, squares(x), pivots_ref[:PANEL, :], lane_squares[...])

    def right_values(columns):
        x = left_ref[...]
        y = pivots_ref[PANEL + columns.start:PANEL + columns.stop, :]
        right_kernels[:, columns] = kernel_values(x, squares(x), y, squares_along_lanes(y))

    def solve(source, high, low, rows, columns):
        inverse = (inverse_high[...], inverse_low[...])
        solved = product(dot_t, split(source[rows, columns]), inverse)
        high[rows, columns], low[rows, columns] = split(solved)
        if rows.start == PANEL:
            low_ref[:, columns] = solved[:local_rows]
            send(low_ref, low_out, columns)

    def reduce(target, high, low, rows, columns, stop, parts=False):
        right = (panel_high[columns, :stop], panel_low[columns, :stop])
        left = (high[rows, :stop], low[rows, :stop])
        values = target[rows, columns] - product(dot_t, left, right)
        if parts:
            high[rows, columns], low[rows, columns] = split(values)
        else:
            target[rows, columns] = values

    def update(at, columns):
        left = (bottom_high[PANEL:, at], bottom_low[PANEL:, at])
        right = (bottom_high[columns, at], bottom_low[columns, at])
        right_kernels[:, columns] = right_kernels[:, columns] - product(dot_t, left, right)

    def later(call, *operands):
        return lambda: call(*operands)

    def assemble(upper, across, lower):
        corner = -product(dot_n, lower, split(product(dot_n, across, upper)))
        low_half, high_half = slice(0, INNER), slice(INNER, OUTER)
        for ref, part, up, down in zip((inverse_high, inverse_low), split(corner), upper, lower):
            ref[low_half, low_half] = up
            ref[low_half, high_half] = jnp.zeros((INNER, INNER), bf16)
            ref[high_half, low_half] = part
            ref[high_half, high_half] = down

    def head_of_next(rows, left_half, right_half, upper, across):
        solved = split(product(dot_t, split(panel[rows, left_half]), upper))
        panel_high[rows, left_half], panel_low[rows, left_half] = solved
        panel[rows, right_half] = panel[rows, right_half] - product(dot_t, solved, across)
        panel[rows, rows] = panel[rows, rows] - product(dot_t, solved, solved)

    def rest_of_next(rows, half, right_half, lower, top):
        solved = split(product(dot_t, split(panel[rows, right_half]), lower))
        panel_high[rows, right_half], panel_low[rows, right_half] = solved
        panel[rows, half] = panel[rows, half] - product(dot_t, solved, top)
        panel[rows, rows] = panel[rows, rows] - product(dot_t, solved, solved)

    arrange(0)
    panel_values(chunks[0])
    carried = []
    block = panel[:INNER, :INNER]
    for step, columns in enumerate(chunks):
        at, mid, end = columns.start, columns.start + INNER, columns.stop
        left_half, right_half = slice(at, mid), slice(mid, end)
        final = step + 1 == len(chunks)
        work = list(carried)
        if step == 0:
            for y in range(1, chips):
                work += [later(arrange, y), later(panel_values, chunks[y])]
            work += [arrange_left]
            work += [later(bottom_values, rows) for rows in bottom_chunks]
            ahead = len(work)
            work += [later(right_values, block_columns) for block_columns in chunks]
        else:
            before = chunks[step - 1]
            work += [later(solve, panel, panel_high, panel_low, rows, before)
                     for rows in chunks[step + 1:]]
            work += [later(reduce, panel, panel_high, panel_low, rows, columns, at)
                     for rows in chunks[step + 1:]]
            if not final:
                work += [later(reduce, panel, panel_high, panel_low, chunks[step + 1],
                               chunks[step + 1], at)]
            ahead = len(work)
            work += [later(solve, bottom, bottom_high, bottom_low, rows, before)
                     for rows in bottom_chunks]
            work += [later(update, before, block_columns) for block_columns in chunks]
            work += [later(reduce, bottom, bottom_high, bottom_low, rows, columns, at, final)
                     for rows in bottom_chunks]
        half = max(ahead, len(work) // 2)
        upper = split(inverse_factor(block, work[:half]))
        work = work[half:]
        across = split(product(dot_t, split(panel[right_half, left_half]), upper))
        block = panel[right_half, right_half] - product(dot_t, across, across)
        if not final:
            rows = chunks[step + 1]
            work = [later(head_of_next, rows, left_half, right_half, upper, across)] + work
        lower = split(inverse_factor(block, work))
        carried = [later(assemble, upper, across, lower)]
        if not final:
            top = slice(rows.start, rows.start + INNER)
            rest = slice(rows.start + INNER, rows.stop)
            solved = split(product(dot_t, split(panel[top, right_half]), lower))
            panel_high[top, right_half], panel_low[top, right_half] = solved
            block = panel[top, top] - product(dot_t, solved, solved)
            carried = [later(rest_of_next, rest, top, right_half, lower, solved)] + carried

    assemble(upper, across, lower)
    columns = chunks[-1]
    inverse = (inverse_high[...], inverse_low[...])
    solved = product(dot_t, (bottom_high[PANEL:, columns], bottom_low[PANEL:, columns]), inverse)
    low_ref[:, columns] = solved[:local_rows]
    send(low_ref, low_out, columns)
    left = split(product(dot_n, split(solved), inverse))
    for rows in chunks:
        values = right_kernels[:, rows] - product(
            dot_t, left, (bottom_high[rows, columns], bottom_low[rows, columns]))
        updated_ref[:, rows] = values[:local_rows]
        send(updated_ref, updated_out, rows)
        own = values[local_rows:local_rows + own_rows]
        row = lax.broadcasted_iota(jnp.int32, own.shape, 0) + offset
        column = lax.broadcasted_iota(jnp.int32, own.shape, 1) + rows.start
        next_ref[:, rows] = own + jnp.where(row == column, RIDGE, 0.0)
    for copy in copies:
        copy.wait()


def local_call(own, same, other, landmarks):
    own_rows = own.shape[1]
    local_rows = landmarks.shape[0]
    left_count = local_rows + 2 * SUB
    total = PANEL + left_count
    return pl.pallas_call(
        local_body,
        out_shape=(
            jax.ShapeDtypeStruct((local_rows, PANEL), f32),
            jax.ShapeDtypeStruct((local_rows, PANEL), f32),
            jax.ShapeDtypeStruct((own_rows, PANEL), f32),
        ),
        scratch_shapes=[
            pltpu.VMEM((PANEL, PANEL), f32),
            pltpu.VMEM((total, PANEL), f32),
            pltpu.VMEM((PANEL, PANEL), bf16),
            pltpu.VMEM((PANEL, PANEL), bf16),
            pltpu.VMEM((total, PANEL), bf16),
            pltpu.VMEM((total, PANEL), bf16),
            pltpu.VMEM((left_count, PANEL), f32),
            pltpu.VMEM((OUTER, OUTER), bf16),
            pltpu.VMEM((OUTER, OUTER), bf16),
            pltpu.VMEM((2 * PANEL, FEAT), bf16),
            pltpu.VMEM((left_count, FEAT), bf16),
            pltpu.VMEM((1, PANEL), f32),
            pltpu.VMEM((local_rows, PANEL), f32),
            pltpu.VMEM((local_rows, PANEL), f32),
            pltpu.SemaphoreType.DMA((2 * PANEL // OUTER,)),
        ],
        out_specs=(
            pl.BlockSpec(memory_space=pl.ANY),
            pl.BlockSpec(memory_space=pl.ANY),
            pl.BlockSpec(memory_space=pltpu.VMEM),
        ),
        compiler_params=pltpu.CompilerParams(vmem_limit_bytes=56 * 1024 * 1024),
        name="panels",
    )(own, same, other, landmarks)


def body(pivots, landmarks):
    own_count, feat = pivots.shape[1:]
    rows, columns = lax.axis_size("row"), lax.axis_size("col")
    chips = rows // CORES
    own = pivots.reshape(2 * own_count, feat)
    groups = [[(y * CORES + core) * columns + c for y in range(chips) for c in range(columns)]
              for core in range(CORES)]
    copies = jnp.broadcast_to(own[None], (chips * columns,) + own.shape)
    same = lax.all_to_all(copies, ("row", "col"), 0, 0, axis_index_groups=groups, tiled=True)
    other = lax.ppermute(same, "row", [(i, i ^ 1) for i in range(rows)])
    return local_call(pivots, same, other, landmarks)


def solution(mesh):
    in_specs = (P(None, ("row", "col"), None), P(("row", "col"), None))
    out_specs = (P(("row", "col"), None), P(("row", "col"), None), P(("row", "col"), None))
    return jax.shard_map(body, mesh=mesh, in_specs=in_specs, out_specs=out_specs, check_vma=False)
```
